32 devices in a mesh: batch: 4 (over z), proto: 8 (over y, x, core).
Axes of the slice: x: 2, y: 2, z: 4, core: 2. Of those that a mesh axis runs over, the one named last changes fastest.
Arguments:
- teacher: bfloat16 [16, 256, 256], P('batch'), may hold values from -1 to 1
- student: bfloat16 [16, 256, 256], P('batch'), may hold values from -0.5 to 0.5
- perm: int32 [16, 256], P('batch'), may hold values from 0 to 255, each once within a row
- counts: int32 [4, 4], P('batch'), may hold values from 1 to 128, 384 in all within a row
- prototypes: bfloat16 [256, 131072], P(None, 'proto'), may hold values from -1 to 1
Outputs:
- feature_grad: float32 [1536, 256], P(('batch', 'proto'))
- proto_grad: float32 [256, 131072], P('batch', 'proto')
The draws below stay inside these ranges and needn't reach their ends.
Inputs may be any that keep to these rules, and one draw needn't show every extreme that they name: Each row of counts sums to exactly 384; some image of each batch index has exactly 128 masked patches. Each row of perm is a permutation of the 256 patches; the first counts entries of an image's row are its masked patches.
All inputs are finite; a program needn't handle non-finite values.
Results may differ from the reference program's by a relative error of at most 0.0053.
Values sent between devices are 32-bit elements; how exact they have to be, the bound alone decides.
A program may use at most 128 MiB of HBM per device.

```python
import math
import jax
import jax.numpy as jnp
import numpy as np
from jax import lax

BOT = 256
K = 131072
P_SIZE = 256
SWEEPS = 3
GROUP_ROWS = 384
IMG_GROUP = 4
IMAGES = 16
ROWS = 1536
N_BATCH = 4


cluster_total = 8


def cluster_signs(key):
    bits = jax.random.randint(jax.random.fold_in(key, 101), (cluster_total, BOT), 0, 2)
    return (bits.astype(jnp.float32) * 2.0 - 1.0) / jnp.sqrt(jnp.float32(BOT))


def draw_teacher(key, part):
    signs = cluster_signs(key)
    first = jax.random.randint(jax.random.fold_in(key, 102), (IMAGES,), 0, cluster_total)
    second = jax.random.randint(jax.random.fold_in(key, 103), (IMAGES,), 0, cluster_total)
    cluster = jnp.minimum(first, second)
    spread = 1.0 / jnp.sqrt(jnp.float32(BOT))
    noise = jax.random.normal(jax.random.fold_in(key, 104), (IMAGES, P_SIZE, BOT), jnp.float32) * spread
    lift = 0.225
    values = lift * signs[cluster][:, None, :] + noise
    return jnp.clip(values, -1.0, 1.0).astype(jnp.bfloat16)


def draw_prototypes(key, part):
    signs = cluster_signs(key)
    column_cluster = jnp.arange(K, dtype=jnp.int32) % cluster_total
    spread = 1.0 / jnp.sqrt(jnp.float32(BOT))
    noise = jax.random.normal(jax.random.fold_in(key, 105), (BOT, K), jnp.float32) * spread
    values = 0.5 * jnp.transpose(signs[column_cluster]) + noise
    return jnp.clip(values, -1.0, 1.0).astype(jnp.bfloat16)


def shard_levels(stream_key, extent, split, least, largest):
    level, own = 1.0, jax.random.fold_in(stream_key, 6)
    for dim, parts in split:
        draws = jnp.exp(jax.random.uniform(jax.random.fold_in(own, dim), (parts,), jnp.float32, least / len(split), largest / len(split)))
        level = level * jnp.repeat(draws, extent[dim] // parts).reshape([-1 if axis == dim else 1 for axis in range(len(extent))])
    return level


def length_profile(number_of, total, bound, lean):
    weights = [(1 << 20) // math.isqrt(grade ** lean) + 1 for grade in range(2, number_of + 1)]
    spare, holding = total - bound - (number_of - 1), [1] * (number_of - 1)
    while spare > 0:
        candidates = [i for i in range(number_of - 1) if holding[i] < bound]
        pool, left = sum([weights[i] for i in candidates]), spare
        for i in candidates:
            more = min(bound - holding[i], max(1, left * weights[i] // pool), spare)
            holding[i] = holding[i] + more
            spare = spare - more
    return np.array([bound] + holding)


def ragged(stream_key, number_of, total, limit, skew):
    if number_of == 2:
        one = jax.random.randint(stream_key, (), max(1, total - limit), min(limit, total - 1) + 1)
        return jnp.stack([one, total - one])
    lengths = jnp.asarray(length_profile(number_of, total, limit, skew), jnp.int32)
    couples = (number_of - 1) // 2
    donor, receiver = lengths[1:1 + 2 * couples:2], lengths[2:2 + 2 * couples:2]
    room = jnp.minimum(donor - 1, limit - receiver)
    moved = jax.random.randint(jax.random.fold_in(stream_key, 1), (couples,), 0, 1 << 20) % (room + 1)
    lengths = lengths.at[1:1 + 2 * couples:2].set(donor - moved).at[2:2 + 2 * couples:2].set(receiver + moved)
    return lengths[jax.random.permutation(jax.random.fold_in(stream_key, 2), number_of)]


def centred(stream_key, extent, width, reach, split=(), kind=jnp.bfloat16):
    array = jax.random.normal(stream_key, extent, jnp.float32) * width
    if len(split) > 0:
        array = shard_levels(stream_key, extent, split, -0.22, 0.18) * array
    return jnp.clip(array, min=-reach, max=reach).astype(kind)


def setup_inputs(seed: int = 0) -> dict:
    arg_keys = jax.random.split(jax.random.key(seed), 6)
    teacher = draw_teacher(jax.random.fold_in(arg_keys[5], 71), 0)
    student = centred(arg_keys[1], (IMAGES, P_SIZE, BOT), 0.0625, 0.5, ((0, 4),))
    perm = jax.vmap(lambda own: jax.random.permutation(own, P_SIZE))(jax.random.split(arg_keys[2], IMAGES)).reshape((IMAGES, P_SIZE)).astype(jnp.int32)
    counts = jax.vmap(lambda own: ragged(own, IMG_GROUP, GROUP_ROWS, P_SIZE // 2, 2))(jax.random.split(arg_keys[3], N_BATCH)).reshape((N_BATCH, IMG_GROUP)).astype(jnp.int32)
    prototypes = draw_prototypes(jax.random.fold_in(arg_keys[5], 71), 0)
    return {"teacher": teacher, "student": student, "perm": perm, "counts": counts, "prototypes": prototypes}


def layout(perm, counts):
    ends = jnp.cumsum(counts, axis=1)
    starts = ends - counts
    line = jnp.arange(GROUP_ROWS, dtype=jnp.int32)
    owner = lax.optimization_barrier(jnp.sum((ends[:, None, :] <= line[None, :, None]).astype(jnp.int32), axis=2))
    first = jnp.take_along_axis(starts, owner, axis=1)
    inner = (line[None, :] - first).astype(jnp.int32)
    image = (owner + (jnp.arange(N_BATCH, dtype=jnp.int32) * IMG_GROUP)[:, None]).astype(jnp.int32)
    patch = perm[image, inner]
    return (image.reshape(-1), patch.reshape(-1))

def unit_rows(rows):
    values = rows.astype(jnp.float32)
    inverse = lax.rsqrt(lax.optimization_barrier(jnp.sum(values * values, axis=1, keepdims=True)) + 1e-06)
    return (values * inverse, inverse)

def reference(teacher, student, perm, counts, prototypes):
    image, patch = layout(perm, counts)
    weight_row = 1.0 / counts.reshape(-1)[image].astype(jnp.float32)
    teach_unit, unused = unit_rows(teacher[image, patch])
    stud_unit, inverse = unit_rows(student[image, patch])
    teach_half = teach_unit.astype(jnp.bfloat16)
    stud_half = stud_unit.astype(jnp.bfloat16)
    energy = jnp.exp(jnp.dot(teach_half, prototypes, preferred_element_type=jnp.float32) * 25.0)
    row_scale = jnp.ones((ROWS,), jnp.float32)
    col_scale = jnp.ones((K,), jnp.float32)
    for sweep in range(SWEEPS):
        col_scale = 1.0 / jnp.dot(row_scale, energy, precision=lax.Precision.HIGHEST)
        row_scale = 1.0 / jnp.dot(energy, col_scale, precision=lax.Precision.HIGHEST)

    def group_step(total, item):
        half, block, scales, weights = item
        expo = jnp.exp(jnp.dot(half, prototypes, preferred_element_type=jnp.float32) * 10.0)
        soft = expo / lax.optimization_barrier(jnp.sum(expo, axis=1, keepdims=True))
        target = scales[:, None] * block * col_scale[None, :]
        grad = (K * 10.0 * weights[:, None] * (soft - target)).astype(jnp.bfloat16)
        total = total + lax.dot_general(half, grad, (((0,), (0,)), ((), ())), preferred_element_type=jnp.float32)
        back = lax.dot_general(grad, prototypes, (((1,), (1,)), ((), ())), preferred_element_type=jnp.float32)
        return (total, back)
    items = (stud_half.reshape(N_BATCH, GROUP_ROWS, BOT), energy.reshape(N_BATCH, GROUP_ROWS, K), row_scale.reshape(N_BATCH, GROUP_ROWS), weight_row.reshape(N_BATCH, GROUP_ROWS))
    proto_grad, back = lax.scan(group_step, jnp.zeros((BOT, K), jnp.float32), items)
    back = back.reshape(ROWS, BOT)
    feature_grad = inverse * (back - stud_unit * lax.optimization_barrier(jnp.sum(stud_unit * back, axis=1, keepdims=True)))
    return (feature_grad, proto_grad)
```

```python
import functools
import math
import jax
import jax.numpy as jnp
from jax import lax
from jax.experimental import pallas as pl
from jax.experimental.pallas import tpu as pltpu
from jax.sharding import PartitionSpec as P

K = 131072
SWEEPS = 3
GROUP_ROWS = 384
LOG2E = 1.4426950408889634
MESH = pl.DeviceIdType.MESH
NT = (((1,), (1,)), ((), ()))


def unit_rows(rows):
    values = rows.astype(jnp.float32)
    inverse = lax.rsqrt(jnp.sum(values * values, axis=1, keepdims=True) + 1e-06)
    return (values * inverse, inverse)


def ring(n, stage, me, buf, send, recv, device):
    copies = []
    for d in range(1, n):
        copies.append(pltpu.make_async_remote_copy(
            src_ref=buf.at[me], dst_ref=buf.at[me], send_sem=send.at[stage, d], recv_sem=recv.at[stage, d],
            device_id=device(lax.rem(me + d, n)), device_id_type=MESH))
    for copy in copies:
        copy.start()
    for copy in copies:
        copy.wait()
    total = buf[0]
    for d in range(1, n):
        total = total + buf[d]
    return total


def scores(weights_t, rows_ref):
    return lax.dot_general(weights_t, rows_ref[...], NT, preferred_element_type=jnp.float32)


def sinkhorn_kernel(nb, np_, cols, step, teach, stud, proto, out, energy, wbuf, tbuf, sbuf, acc, acc2, wsem,
                    p0, p1, p2, q0, q1, q2, psend, precv, qsend, qrecv):
    b, p = lax.axis_index("batch"), lax.axis_index("proto")
    rows = teach.shape[0]
    load = pltpu.make_async_copy(proto.at[:, pl.ds(pl.multiple_of(b * cols, cols), cols)], wbuf, wsem)
    load.start()
    barrier = pltpu.get_barrier_semaphore()
    for d in range(1, np_):
        pl.semaphore_signal(barrier, inc=1, device_id=(b, lax.rem(p + d, np_)), device_id_type=MESH)
    for d in range(1, nb):
        pl.semaphore_signal(barrier, inc=1, device_id=(lax.rem(b + d, nb), p), device_id_type=MESH)
    pl.semaphore_wait(barrier, np_ + nb - 2)
    load.wait()
    acc[...] = jnp.zeros_like(acc)
    acc2[...] = jnp.zeros_like(acc2)

    def first(i, carry):
        wt = wbuf[:, pl.ds(pl.multiple_of(i * step, step), step)].T
        tbuf[...] = scores(wt, teach)
        sbuf[...] = scores(wt, stud)
        row = acc[...]
        row2 = acc2[...]
        for g in range(0, step, 8):
            e = jnp.exp2(tbuf[g:g + 8, :] * (25.0 * LOG2E))
            energy[pl.ds(pl.multiple_of(i * step + g, 8), 8), :] = e
            row = row + e * (1.0 / jnp.sum(e, axis=1, keepdims=True))
            row2 = row2 + jnp.exp2(sbuf[g:g + 8, :] * (10.0 * LOG2E))
        acc[...] = row
        acc2[...] = row2
        return carry

    lax.fori_loop(0, cols // step, first, 0)

    def reduce(stage, value, pbuf, qbuf):
        pbuf[p] = value
        part = ring(np_, stage, p, pbuf, psend, precv, lambda other: (b, other))
        qbuf[b] = part
        return ring(nb, stage, b, qbuf, qsend, qrecv, lambda other: (other, p))

    value = jnp.concatenate([jnp.sum(acc[...], axis=0, keepdims=True), jnp.sum(acc2[...], axis=0, keepdims=True)], axis=1)
    total = reduce(0, value, p0, q0)
    out[0:1, :] = total[:, rows:]
    scale = 1.0 / total[:, :rows]
    for sweep in range(1, SWEEPS):
        out[2 * sweep - 1:2 * sweep, :] = scale
        wide = jnp.broadcast_to(scale, (8, rows))

        def body(i, row):
            for g in range(0, 128, 8):
                e = energy[pl.ds(pl.multiple_of(i * 128 + g, 8), 8), :]
                row = row + e * (1.0 / jnp.sum(e * wide, axis=1, keepdims=True))
            return row

        row = lax.fori_loop(0, cols // 128, body, jnp.zeros((8, rows), jnp.float32))
        total = reduce(sweep, jnp.sum(row, axis=0, keepdims=True), (p0, p1, p2)[sweep], (q0, q1, q2)[sweep])
        scale = 1.0 / total
    out[2 * SWEEPS - 1:2 * SWEEPS, :] = scale


def gradient_kernel(nb, np_, half, step, share, teach, stud, stud_t, vec, proto, out, back_out,
                    wbuf, tbuf, sbuf, gbuf, own, away, back, parts, mine_buf, wsem, osem, asend, arecv, bsend, brecv):
    b, p = lax.axis_index("batch"), lax.axis_index("proto")
    rows = teach.shape[0]
    h = lax.rem(b, 2)
    pair = b - h
    other = pair + 1 - h
    pair_rows = 2 * np_ * share
    block = out.shape[0]
    base = h * half
    load = pltpu.make_async_copy(proto.at[:, pl.ds(pl.multiple_of(base, half), half)], wbuf, wsem)
    load.start()
    barrier = pltpu.get_barrier_semaphore()
    for d in range(1, np_):
        peer = lax.rem(p + d, np_)
        pl.semaphore_signal(barrier, inc=1, device_id=(b, peer), device_id_type=MESH)
        pl.semaphore_signal(barrier, inc=1, device_id=(other, peer), device_id_type=MESH)
    pl.semaphore_signal(barrier, inc=1, device_id=(other, p), device_id_type=MESH)
    pl.semaphore_wait(barrier, 2 * np_ - 1)
    load.wait()
    back[...] = jnp.zeros_like(back)
    scale_prev, target_scale, soft_scale = vec[0:1, :], vec[1:2, :], vec[2:3, :]

    def body(i, carry):
        cols = pl.ds(pl.multiple_of(i * step, step), step)
        w = wbuf[:, cols]
        wt = w.T
        tbuf[...] = scores(wt, teach)
        sbuf[...] = scores(wt, stud)
        for g in range(0, step, 16):
            e = jnp.exp2(tbuf[g:g + 16, :] * (25.0 * LOG2E))
            c = 1.0 / jnp.sum(e * scale_prev, axis=1, keepdims=True)
            soft = jnp.exp2(sbuf[g:g + 16, :] * (10.0 * LOG2E)) * soft_scale
            gbuf[g:g + 16, :] = (soft - e * target_scale * c).astype(jnp.bfloat16)
        res = lax.dot_general(stud_t[...], gbuf[...], NT, preferred_element_type=jnp.float32)
        own[:, cols] = res[:block]
        away[:, cols] = res[block:]
        there = pl.ds(pl.multiple_of(base + i * step, step), step)
        pltpu.make_async_remote_copy(
            src_ref=away.at[:, cols], dst_ref=out.at[:, there], send_sem=asend, recv_sem=arecv,
            device_id=(other, p), device_id_type=MESH).start()
        pltpu.make_async_copy(own.at[:, cols], out.at[:, there], osem).start()
        part = gbuf[:, pl.ds(pl.multiple_of((b // 2) * pair_rows, pair_rows), pair_rows)]
        back[...] += jnp.dot(w, part, preferred_element_type=jnp.float32)
        return carry

    lax.fori_loop(0, half // step, body, 0)
    full = back[...].T
    for s in range(2 * np_):
        parts[s, 0:share, :] = full[s * share:(s + 1) * share, :]
    copies = []
    slot = h * np_ + p
    for d in range(1, 2 * np_):
        to = lax.rem(slot + d, 2 * np_)
        copies.append(pltpu.make_async_remote_copy(
            src_ref=parts.at[to], dst_ref=mine_buf.at[d],
            send_sem=bsend.at[d], recv_sem=brecv.at[d],
            device_id=(pair + to // np_, lax.rem(to, np_)), device_id_type=MESH))
    for copy in copies:
        copy.start()
    total = parts[slot]
    for copy in copies:
        copy.wait()
    for d in range(1, 2 * np_):
        total = total + mine_buf[d]
    back_out[...] = total[:share]
    there = pl.ds(pl.multiple_of(base, half), half)
    pltpu.make_async_copy(own, out.at[:, there], osem).wait()
    arrive = pl.ds(pl.multiple_of(half - base, half), half)
    whole = pltpu.make_async_remote_copy(
        src_ref=away, dst_ref=out.at[:, arrive], send_sem=asend, recv_sem=arecv,
        device_id=(other, p), device_id_type=MESH)
    whole.wait()


def on_device(nb, np_, teacher, student, perm, counts, prototypes):
    img_count = teacher.shape[0]
    patches = teacher.shape[1]
    width = teacher.shape[2]
    group_rows = GROUP_ROWS
    rows = nb * group_rows
    share = group_rows // np_
    local = prototypes.shape[1]
    b, p = lax.axis_index("batch"), lax.axis_index("proto")
    tally = counts.reshape(-1)
    ends = jnp.cumsum(tally)
    starts = ends - tally
    line = p * share + jnp.arange(share, dtype=jnp.int32)
    owner = jnp.sum((ends[None, :] <= line[:, None]).astype(jnp.int32), axis=1)
    picked = owner[:, None] == jnp.arange(img_count, dtype=jnp.int32)[None, :]
    first = jnp.sum(jnp.where(picked, starts[None, :], 0), axis=1)
    owned = jnp.sum(jnp.where(picked, tally[None, :], 0), axis=1)
    inner = line - first
    flat = owner * patches + jnp.take(perm.reshape(-1), owner * patches + inner)
    teach_unit, unused = unit_rows(jnp.take(teacher.reshape(-1, width), flat, axis=0))
    own_unit, own_inverse = unit_rows(jnp.take(student.reshape(-1, width), flat, axis=0))
    weight = jnp.broadcast_to((K * 10.0) * (1.0 / owned.astype(jnp.float32))[:, None], (share, 128))
    packed = jnp.concatenate(
        [teach_unit.astype(jnp.bfloat16).astype(jnp.float32), own_unit.astype(jnp.bfloat16).astype(jnp.float32), weight], axis=1)
    gathered = lax.all_gather(packed, ("batch", "proto"), axis=0, tiled=True)
    teach = gathered[:, :width].astype(jnp.bfloat16)
    stud = gathered[:, width:2 * width].astype(jnp.bfloat16)
    weight_row = gathered[:, 2 * width].reshape(1, rows)

    cols = local // nb
    step = min(256, cols)
    vmem = pltpu.VMEM
    f32 = jnp.float32
    dma = pltpu.SemaphoreType.DMA
    whole = pl.BlockSpec(memory_space=vmem)
    sums = pl.pallas_call(
        functools.partial(sinkhorn_kernel, nb, np_, cols, step),
        out_shape=jax.ShapeDtypeStruct((8, rows), f32),
        in_specs=[whole, whole, pl.BlockSpec(memory_space=pl.ANY)],
        out_specs=whole,
        scratch_shapes=[
            vmem((cols, rows), f32), vmem((width, cols), jnp.bfloat16), vmem((step, rows), f32), vmem((step, rows), f32),
            vmem((8, rows), f32), vmem((8, rows), f32), dma,
            vmem((np_, 1, 2 * rows), f32), vmem((np_, 1, rows), f32), vmem((np_, 1, rows), f32),
            vmem((nb, 1, 2 * rows), f32), vmem((nb, 1, rows), f32), vmem((nb, 1, rows), f32),
            dma((SWEEPS, np_)), dma((SWEEPS, np_)), dma((SWEEPS, nb)), dma((SWEEPS, nb)),
        ],
        compiler_params=pltpu.CompilerParams(collective_id=0, has_side_effects=True, vmem_limit_bytes=56 * 2**20),
        name="sinkhorn",
    )(teach, stud, prototypes)
    vec = jnp.concatenate(
        [sums[3:4], sums[5:6] * weight_row, weight_row / sums[0:1], jnp.zeros((5, rows), f32)], axis=0)

    half = local // 2
    step2 = min(256, half)
    block = width // nb
    stud_cols = stud.T
    other = b + 1 - 2 * lax.rem(b, 2)
    stud_t = jnp.concatenate([
        lax.dynamic_slice_in_dim(stud_cols, b * block, block, 0),
        lax.dynamic_slice_in_dim(stud_cols, other * block, block, 0)], axis=0)
    pair_rows = 2 * group_rows
    pad = -(-share // 8) * 8
    proto_grad, back = pl.pallas_call(
        functools.partial(gradient_kernel, nb, np_, half, step2, share),
        out_shape=[jax.ShapeDtypeStruct((block, local), f32), jax.ShapeDtypeStruct((share, width), f32)],
        in_specs=[whole, whole, whole, whole, pl.BlockSpec(memory_space=pl.ANY)],
        out_specs=[pl.BlockSpec(memory_space=pl.ANY), whole],
        scratch_shapes=[
            vmem((width, half), jnp.bfloat16), vmem((step2, rows), f32), vmem((step2, rows), f32),
            vmem((step2, rows), jnp.bfloat16), vmem((block, half), f32), vmem((block, half), f32),
            vmem((width, pair_rows), f32), vmem((2 * np_, pad, width), f32), vmem((2 * np_, pad, width), f32),
            dma, dma, dma, dma, dma((2 * np_,)), dma((2 * np_,)),
        ],
        compiler_params=pltpu.CompilerParams(collective_id=1, has_side_effects=True, vmem_limit_bytes=56 * 2**20),
        name="gradient",
    )(teach, stud, stud_t, vec, prototypes)
    feature_grad = own_inverse * (back - own_unit * jnp.sum(own_unit * back, axis=1, keepdims=True))
    return (feature_grad, proto_grad)


def solution(mesh):
    in_specs = (
        P("batch", None, None),
        P("batch", None, None),
        P("batch", None),
        P("batch", None),
        P(None, "proto"),
    )
    out_specs = (P(("batch", "proto"), None), P("batch", "proto"))
    run = functools.partial(on_device, mesh.shape["batch"], mesh.shape["proto"])
    return jax.shard_map(run, mesh=mesh, in_specs=in_specs, out_specs=out_specs, check_vma=False)
```

```python
import functools
import jax
import jax.numpy as jnp
from jax import lax
from jax.experimental import pallas as pl
from jax.experimental.pallas import tpu as pltpu
from jax.sharding import PartitionSpec as P

K = 131072
SWEEPS = 3
GROUP_ROWS = 384
LOG2E = 1.4426950408889634
MESH = pl.DeviceIdType.MESH
NT = (((1,), (1,)), ((), ()))


def unit_rows(rows):
    values = rows.astype(jnp.float32)
    inverse = lax.rsqrt(jnp.sum(values * values, axis=1, keepdims=True) + 1e-06)
    return (values * inverse, inverse)


def flip(index, bit):
    size = 2 ** bit
    return index + size - 2 * size * lax.rem(index // size, 2)


def dot_nt(left, right):
    return lax.dot_general(left, right, NT, preferred_element_type=jnp.float32)


def head_kernel(nb, np_, share, cols, step, teach_own, stud_own, weight_own, proto, out, back_out,
                teach_buf, stud_buf, weight_buf, teach, stud, stud_t, stage, energy, wbuf, ta, tb, sa, sb, ga, gb,
                acc, acc2, own, away, back, parts, mine_buf, p0, p1, p2, q0, q1, q2,
                wsem, osem, asend, arecv, bsend, brecv, psend, precv, qsend, qrecv,
                zsend, zrecv, gsend, grecv):
    b, p = lax.axis_index("batch"), lax.axis_index("proto")
    rows = teach.shape[0]
    group_rows = rows // nb
    bits = np_.bit_length() - 1
    h = lax.rem(b, 2)
    pair = b - h
    other = pair + 1 - h
    quarters = nb // 2
    mine = b // 2
    half = cols * quarters
    base = h * half
    block = out.shape[0]
    pair_rows = 2 * group_rows
    chunks = cols // step
    load = pltpu.make_async_copy(proto.at[:, pl.ds(pl.multiple_of(base, half), half)], wbuf, wsem)
    load.start()
    barrier = pltpu.get_barrier_semaphore()
    for d in range(1, np_):
        peer = lax.rem(p + d, np_)
        pl.semaphore_signal(barrier, inc=1, device_id=(b, peer), device_id_type=MESH)
        pl.semaphore_signal(barrier, inc=1, device_id=(other, peer), device_id_type=MESH)
    for d in range(1, nb):
        pl.semaphore_signal(barrier, inc=1, device_id=(lax.rem(b + d, nb), p), device_id_type=MESH)
    teach_buf[p, b] = teach_own[...]
    stud_buf[p, b] = stud_own[...]
    weight_buf[b] = weight_own[...]
    pl.semaphore_wait(barrier, 2 * (np_ - 1) + nb - 1)

    def along_batch(which, ref):
        copies = []
        for d in range(1, nb):
            copies.append(pltpu.make_async_remote_copy(
                src_ref=ref, dst_ref=ref, send_sem=zsend.at[which, d], recv_sem=zrecv.at[which, d],
                device_id=(lax.rem(b + d, nb), p), device_id_type=MESH))
        for copy in copies:
            copy.start()
        return copies

    def along_proto(which, buf, number):
        copies = []
        for part in range(2):
            outer = list(range(1, bits))
            order = (outer if part == 0 else outer[::-1]) + [0]
            held = [p]
            for bit in order[:number]:
                held = held + [flip(q, bit) for q in held]
            for k, slot in enumerate(held):
                ref = buf.at[slot, pl.ds(part * (nb // 2), nb // 2)]
                at = 2 ** number - 1 + k
                copies.append(pltpu.make_async_remote_copy(
                    src_ref=ref, dst_ref=ref, send_sem=gsend.at[which, part, at], recv_sem=grecv.at[which, part, at],
                    device_id=(b, flip(p, order[number])), device_id_type=MESH))
        for copy in copies:
            copy.start()
        return copies

    def finish(copies):
        for copy in copies:
            copy.wait()

    def round_rows(buf, target):
        for i in range(nb):
            for q in range(np_):
                stage[q * share:(q + 1) * share, :] = buf[q, i, 0:share, :]
            target[i * group_rows:(i + 1) * group_rows, :] = stage[...].astype(jnp.bfloat16)

    teach_moves = along_batch(0, teach_buf.at[p, b])
    stud_moves = along_batch(1, stud_buf.at[p, b])
    weight_moves = along_batch(2, weight_buf.at[b])
    for number in range(bits):
        finish(teach_moves)
        teach_moves = along_proto(0, teach_buf, number)
    load.wait()
    finish(stud_moves)
    finish(teach_moves)
    stud_moves = along_proto(1, stud_buf, 0)
    round_rows(teach_buf, teach)
    acc[...] = jnp.zeros_like(acc)
    acc2[...] = jnp.zeros_like(acc2)
    back[...] = jnp.zeros_like(back)

    def columns(quarter, i):
        return pl.ds(pl.multiple_of(quarter * cols + i * step, step), step)

    def pick(quarter, i):
        return wbuf[:, columns(quarter, i)].T

    def loop(low, high, one):
        if (high - low) % 2 == 0:
            def body(j, carry):
                one(low + 2 * j, 0)
                one(low + 2 * j + 1, 1)
                return carry
            lax.fori_loop(0, (high - low) // 2, body, 0)
        else:
            def body(j, carry):
                one(low + j, 0)
                return carry
            lax.fori_loop(0, high - low, body, 0)

    tbufs, sbufs, gbufs = (ta, tb), (sa, sb), (ga, gb)

    def teach_chunk(i, which):
        buf = tbufs[which]
        buf[...] = dot_nt(pick(mine, i), teach[...])
        row = acc[...]
        for g in range(0, step, 8):
            e = jnp.exp2(buf[g:g + 8, :] * (25.0 * LOG2E))
            energy[pl.ds(pl.multiple_of(i * step + g, 8), 8), :] = e
            row = row + e * (1.0 / jnp.sum(e, axis=1, keepdims=True))
        acc[...] = row

    def stud_chunk(i, which):
        buf = sbufs[which]
        buf[...] = dot_nt(pick(mine, i), stud[...])
        row = acc2[...]
        for g in range(0, step, 8):
            row = row + jnp.exp2(buf[g:g + 8, :] * (10.0 * LOG2E))
        acc2[...] = row

    for number in range(bits):
        loop(chunks * number // bits, chunks * (number + 1) // bits, teach_chunk)
        finish(stud_moves)
        if number + 1 < bits:
            stud_moves = along_proto(1, stud_buf, number + 1)
    round_rows(stud_buf, stud)
    stud_t[...] = stud[...].T
    finish(weight_moves)
    weight = jnp.concatenate([weight_buf[i] for i in range(nb)], axis=1)

    def reduce(sweep, value, pbuf, qbuf, beside):
        pbuf[p] = value
        copies = []
        for d in range(1, np_):
            copies.append(pltpu.make_async_remote_copy(
                src_ref=pbuf.at[p], dst_ref=pbuf.at[p], send_sem=psend.at[sweep, d], recv_sem=precv.at[sweep, d],
                device_id=(b, lax.rem(p + d, np_)), device_id_type=MESH))
        for copy in copies:
            copy.start()
        beside(2 * sweep)
        finish(copies)
        total = pbuf[0]
        for d in range(1, np_):
            total = total + pbuf[d]
        qbuf[b] = total
        copies = []
        for d in range(1, nb):
            copies.append(pltpu.make_async_remote_copy(
                src_ref=qbuf.at[b], dst_ref=qbuf.at[b], send_sem=qsend.at[sweep, d], recv_sem=qrecv.at[sweep, d],
                device_id=(lax.rem(b + d, nb), p), device_id_type=MESH))
        for copy in copies:
            copy.start()
        beside(2 * sweep + 1)
        finish(copies)
        total = qbuf[0]
        for d in range(1, nb):
            total = total + qbuf[d]
        return total

    gaps = 2 * (SWEEPS - 1)

    def beside(gap):
        if gap < gaps:
            loop(chunks * gap // gaps, chunks * (gap + 1) // gaps, stud_chunk)

    scale = 1.0 / reduce(0, jnp.sum(acc[...], axis=0, keepdims=True), p0, q0, beside)
    for sweep in range(1, SWEEPS):
        last = scale
        wide = jnp.broadcast_to(scale, (8, rows))

        def body(i, row):
            for g in range(0, 128, 8):
                e = energy[pl.ds(pl.multiple_of(i * 128 + g, 8), 8), :]
                row = row + e * (1.0 / jnp.sum(e * wide, axis=1, keepdims=True))
            return row

        row = jnp.sum(lax.fori_loop(0, cols // 128, body, jnp.zeros((8, rows), jnp.float32)), axis=0, keepdims=True)
        if sweep == SWEEPS - 1:
            row = jnp.concatenate([row, jnp.sum(acc2[...], axis=0, keepdims=True)], axis=1)
        total = reduce(sweep, row, (p0, p1, p2)[sweep], (q0, q1, q2)[sweep], beside)
        scale = 1.0 / total[:, :rows]
    acc[0:1, :] = last
    acc[1:2, :] = scale * weight
    acc[2:3, :] = weight / total[:, rows:]
    scale_prev, target_scale, soft_scale = acc[0:1, :], acc[1:2, :], acc[2:3, :]
    keep = stud_t[pl.ds(pl.multiple_of(mine * 2 * block, 2 * block), 2 * block), :]

    def send(quarter, i):
        at = columns(quarter, i)
        there = pl.ds(pl.multiple_of(base + quarter * cols + i * step, step), step)
        pltpu.make_async_remote_copy(
            src_ref=away.at[:, at], dst_ref=out.at[:, there], send_sem=asend, recv_sem=arecv,
            device_id=(other, p), device_id_type=MESH).start()
        pltpu.make_async_copy(own.at[:, at], out.at[:, there], osem).start()

    def gradient(quarter, i, which, known):
        s, t, grad = sbufs[which], tbufs[which], gbufs[which]
        for g in range(0, step, 16):
            if known:
                e = energy[pl.ds(pl.multiple_of(i * step + g, 16), 16), :]
            else:
                e = jnp.exp2(t[g:g + 16, :] * (25.0 * LOG2E))
            c = 1.0 / jnp.sum(e * scale_prev, axis=1, keepdims=True)
            soft = jnp.exp2(s[g:g + 16, :] * (10.0 * LOG2E)) * soft_scale
            grad[g:g + 16, :] = (soft - e * target_scale * c).astype(jnp.bfloat16)

    def products(quarter, i, which):
        at = columns(quarter, i)
        grad = gbufs[which]
        res = dot_nt(keep, grad[...])
        low, high = res[:block], res[block:]
        own[:, at] = jnp.where(h == 0, low, high)
        away[:, at] = jnp.where(h == 0, high, low)
        part = grad[:, pl.ds(pl.multiple_of(mine * pair_rows, pair_rows), pair_rows)]
        back[...] += jnp.dot(wbuf[:, at], part, preferred_element_type=jnp.float32)

    def prepare(quarter, i, which, known):
        wt = pick(quarter, i)
        sbufs[which][...] = dot_nt(wt, stud[...])
        if not known:
            tbufs[which][...] = dot_nt(wt, teach[...])

    for turn in range(quarters):
        quarter = lax.rem(mine + turn, quarters)
        known = turn == 0
        if chunks % 2 == 0:
            prepare(quarter, 0, 0, known)

            def body(j, carry):
                i = 2 * j
                prepare(quarter, i + 1, 1, known)
                gradient(quarter, i, 0, known)
                products(quarter, i, 0)
                prepare(quarter, lax.rem(i + 2, chunks), 0, known)
                gradient(quarter, i + 1, 1, known)
                products(quarter, i + 1, 1)
                send(quarter, i)
                send(quarter, i + 1)
                return carry

            lax.fori_loop(0, chunks // 2, body, 0)
        else:
            def body(i, carry):
                prepare(quarter, i, 0, known)
                gradient(quarter, i, 0, known)
                products(quarter, i, 0)
                send(quarter, i)
                return carry

            lax.fori_loop(0, chunks, body, 0)

    full = back[...].T
    for s in range(2 * np_):
        parts[s, 0:share, :] = full[s * share:(s + 1) * share, :]
    copies = []
    slot = h * np_ + p
    for d in range(1, 2 * np_):
        to = lax.rem(slot + d, 2 * np_)
        copies.append(pltpu.make_async_remote_copy(
            src_ref=parts.at[to], dst_ref=mine_buf.at[d], send_sem=bsend.at[d], recv_sem=brecv.at[d],
            device_id=(pair + to // np_, lax.rem(to, np_)), device_id_type=MESH))
    for copy in copies:
        copy.start()
    total = parts[slot]
    finish(copies)
    for d in range(1, 2 * np_):
        total = total + mine_buf[d]
    back_out[...] = total[:share]
    there = pl.ds(pl.multiple_of(base, half), half)
    pltpu.make_async_copy(own, out.at[:, there], osem).wait()
    arrive = pl.ds(pl.multiple_of(half - base, half), half)
    pltpu.make_async_remote_copy(
        src_ref=away, dst_ref=out.at[:, arrive], send_sem=asend, recv_sem=arecv,
        device_id=(other, p), device_id_type=MESH).wait()


def on_device(nb, np_, teacher, student, perm, counts, prototypes):
    img_count = teacher.shape[0]
    patches = teacher.shape[1]
    width = teacher.shape[2]
    group_rows = GROUP_ROWS
    rows = nb * group_rows
    share = group_rows // np_
    pad = -(-share // 8) * 8
    local = prototypes.shape[1]
    p = lax.axis_index("proto")
    tally = counts.reshape(-1)
    ends = jnp.cumsum(tally)
    starts = ends - tally
    line = jnp.arange(group_rows, dtype=jnp.int32)
    owner = jnp.sum((ends[None, :] <= line[:, None]).astype(jnp.int32), axis=1)
    picked = owner[:, None] == jnp.arange(img_count, dtype=jnp.int32)[None, :]
    first = jnp.sum(jnp.where(picked, starts[None, :], 0), axis=1)
    owned = jnp.sum(jnp.where(picked, tally[None, :], 0), axis=1)
    weight = ((K * 10.0) * (1.0 / owned.astype(jnp.float32))).reshape(1, group_rows)
    place = lax.dynamic_slice_in_dim(owner * patches + line - first, p * share, share, 0)
    image = lax.dynamic_slice_in_dim(owner * patches, p * share, share, 0)
    flat = image + jnp.take(perm.reshape(-1), place)
    teach_unit, unused = unit_rows(jnp.take(teacher.reshape(-1, width), flat, axis=0))
    own_unit, own_inverse = unit_rows(jnp.take(student.reshape(-1, width), flat, axis=0))
    fill = lambda x: jnp.pad(x, ((0, pad - share), (0, 0))) if pad > share else x

    cols = local // nb
    step = min(256, cols)
    half = local // 2
    block = width // nb
    pair_rows = 2 * group_rows
    vmem = pltpu.VMEM
    f32, bf16 = jnp.float32, jnp.bfloat16
    dma = pltpu.SemaphoreType.DMA
    whole = pl.BlockSpec(memory_space=vmem)
    proto_grad, back = pl.pallas_call(
        functools.partial(head_kernel, nb, np_, share, cols, step),
        out_shape=[jax.ShapeDtypeStruct((block, local), f32), jax.ShapeDtypeStruct((share, width), f32)],
        in_specs=[whole, whole, whole, pl.BlockSpec(memory_space=pl.ANY)],
        out_specs=[pl.BlockSpec(memory_space=pl.ANY), whole],
        scratch_shapes=[
            vmem((np_, nb, pad, width), f32), vmem((np_, nb, pad, width), f32), vmem((nb, 1, group_rows), f32),
            vmem((rows, width), bf16), vmem((rows, width), bf16), vmem((width, rows), bf16),
            vmem((group_rows, width), f32), vmem((cols, rows), f32), vmem((width, half), bf16),
            vmem((step, rows), f32), vmem((step, rows), f32), vmem((step, rows), f32), vmem((step, rows), f32),
            vmem((step, rows), bf16), vmem((step, rows), bf16),
            vmem((8, rows), f32), vmem((8, rows), f32),
            vmem((block, half), f32), vmem((block, half), f32),
            vmem((width, pair_rows), f32), vmem((2 * np_, pad, width), f32), vmem((2 * np_, pad, width), f32),
            vmem((np_, 1, rows), f32), vmem((np_, 1, rows), f32), vmem((np_, 1, 2 * rows), f32),
            vmem((nb, 1, rows), f32), vmem((nb, 1, rows), f32), vmem((nb, 1, 2 * rows), f32),
            dma, dma, dma, dma, dma((2 * np_,)), dma((2 * np_,)),
            dma((SWEEPS, np_)), dma((SWEEPS, np_)), dma((SWEEPS, nb)), dma((SWEEPS, nb)),
            dma((3, nb)), dma((3, nb)), dma((2, 2, np_)), dma((2, 2, np_)),
        ],
        compiler_params=pltpu.CompilerParams(collective_id=0, has_side_effects=True, vmem_limit_bytes=60 * 2**20),
        name="head",
    )(fill(teach_unit), fill(own_unit), weight, prototypes)
    feature_grad = own_inverse * (back - own_unit * jnp.sum(own_unit * back, axis=1, keepdims=True))
    return (feature_grad, proto_grad)


def solution(mesh):
    in_specs = (
        P("batch", None, None),
        P("batch", None, None),
        P("batch", None),
        P("batch", None),
        P(None, "proto"),
    )
    out_specs = (P(("batch", "proto"), None), P("batch", "proto"))
    run = functools.partial(on_device, mesh.shape["batch"], mesh.shape["proto"])
    return jax.shard_map(run, mesh=mesh, in_specs=in_specs, out_specs=out_specs, check_vma=False)
```

```python
import functools
import jax
import jax.numpy as jnp
from jax import lax
from jax.experimental import pallas as pl
from jax.experimental.pallas import tpu as pltpu
from jax.sharding import PartitionSpec as P

K = 131072
SWEEPS = 3
GROUP_ROWS = 384
LOG2E = 1.4426950408889634
MESH = pl.DeviceIdType.MESH
NT = (((1,), (1,)), ((), ()))


def unit_rows(rows):
    values = rows.astype(jnp.float32)
    inverse = lax.rsqrt(jnp.sum(values * values, axis=1, keepdims=True) + 1e-06)
    return (values * inverse, inverse)


def flip(index, bit):
    size = 2 ** bit
    return index + size - 2 * size * lax.rem(index // size, 2)


def dot_nt(left, right):
    return lax.dot_general(left, right, NT, preferred_element_type=jnp.float32)


def head_kernel(nb, np_, share, cols, step, twice, teach_own, stud_own, inverse, weight_own, proto, out, feature,
                teach_buf, stud_buf, weight_buf, teach, stud, stud_t, stage, energy, wbuf, ta, tb, sa, sb, ga, gb,
                acc, acc2, own, away, back, parts, mine_buf, p0, p1, p2, q0, q1, q2,
                wsem, osem, asend, arecv, bsend, brecv, psend, precv, qsend, qrecv,
                zsend, zrecv, gsend, grecv):
    b, p = lax.axis_index("batch"), lax.axis_index("proto")
    rows = teach.shape[0]
    group_rows = rows // nb
    bits = np_.bit_length() - 1
    h = lax.rem(b, 2)
    pair = b - h
    other = pair + 1 - h
    quarters = nb // 2
    mine = b // 2
    half = cols * quarters
    base = h * half
    block = out.shape[0]
    pair_rows = 2 * group_rows
    chunks = cols // step
    load = pltpu.make_async_copy(proto, wbuf, wsem)
    load.start()
    barrier = pltpu.get_barrier_semaphore()
    for d in range(1, np_):
        peer = lax.rem(p + d, np_)
        pl.semaphore_signal(barrier, inc=1, device_id=(b, peer), device_id_type=MESH)
        pl.semaphore_signal(barrier, inc=1, device_id=(other, peer), device_id_type=MESH)
    for d in range(1, nb):
        pl.semaphore_signal(barrier, inc=1, device_id=(lax.rem(b + d, nb), p), device_id_type=MESH)
    teach_buf[p, b] = teach_own[...]
    stud_buf[p, b] = stud_own[...]
    weight_buf[b] = weight_own[...]
    pl.semaphore_wait(barrier, 2 * (np_ - 1) + nb - 1)

    def along_batch(which, ref):
        copies = []
        for d in range(1, nb):
            copies.append(pltpu.make_async_remote_copy(
                src_ref=ref, dst_ref=ref, send_sem=zsend.at[which, d], recv_sem=zrecv.at[which, d],
                device_id=(lax.rem(b + d, nb), p), device_id_type=MESH))
        for copy in copies:
            copy.start()
        return copies

    def along_proto(which, buf, number):
        copies = []
        for part in range(2):
            outer = list(range(1, bits))
            order = (outer if part == 0 else outer[::-1]) + [0]
            held = [p]
            for bit in order[:number]:
                held = held + [flip(q, bit) for q in held]
            for k, slot in enumerate(held):
                ref = buf.at[slot, pl.ds(part * (nb // 2), nb // 2)]
                at = 2 ** number - 1 + k
                copies.append(pltpu.make_async_remote_copy(
                    src_ref=ref, dst_ref=ref, send_sem=gsend.at[which, part, at], recv_sem=grecv.at[which, part, at],
                    device_id=(b, flip(p, order[number])), device_id_type=MESH))
        for copy in copies:
            copy.start()
        return copies

    def finish(copies):
        for copy in copies:
            copy.wait()

    def round_rows(buf, target):
        for i in range(nb):
            for q in range(np_):
                stage[q * share:(q + 1) * share, :] = buf[q, i, 0:share, :]
            target[i * group_rows:(i + 1) * group_rows, :] = stage[...].astype(jnp.bfloat16)

    teach_moves = along_batch(0, teach_buf.at[p, b])
    for number in range(bits):
        finish(teach_moves)
        teach_moves = along_proto(0, teach_buf, number)
        if number == 0:
            stud_moves = along_batch(1, stud_buf.at[p, b])
            weight_moves = along_batch(2, weight_buf.at[b])
    load.wait()
    finish(stud_moves)
    finish(teach_moves)
    stud_moves = along_proto(1, stud_buf, 0)
    round_rows(teach_buf, teach)
    acc[...] = jnp.zeros_like(acc)
    acc2[...] = jnp.zeros_like(acc2)
    back[...] = jnp.zeros_like(back)

    def columns(start, i):
        return pl.ds(pl.multiple_of(start + i * step, step), step)

    def pick(start, i):
        return wbuf[:, columns(start, i)].T

    first = base + mine * cols

    def loop(low, high, one):
        if (high - low) % 2 == 0:
            def body(j, carry):
                one(low + 2 * j, 0)
                one(low + 2 * j + 1, 1)
                return carry
            lax.fori_loop(0, (high - low) // 2, body, 0)
        else:
            def body(j, carry):
                one(low + j, 0)
                return carry
            lax.fori_loop(0, high - low, body, 0)

    tbufs, sbufs, gbufs = (ta, tb), (sa, sb), (ga, gb)

    def teach_chunk(i, which):
        buf = tbufs[which]
        buf[...] = dot_nt(pick(first, i), teach[...])
        row = acc[...]
        for g in range(0, step, 8):
            e = jnp.exp2(buf[g:g + 8, :] * (25.0 * LOG2E))
            energy[pl.ds(pl.multiple_of(i * step + g, 8), 8), :] = e
            row = row + e * (1.0 / jnp.sum(e, axis=1, keepdims=True))
        acc[...] = row

    def stud_chunk(i, which):
        buf = sbufs[which]
        buf[...] = dot_nt(pick(first, i), stud[...])
        row = acc2[...]
        for g in range(0, step, 8):
            row = row + jnp.exp2(buf[g:g + 8, :] * (10.0 * LOG2E))
        acc2[...] = row

    for number in range(bits):
        loop(chunks * number // bits, chunks * (number + 1) // bits, teach_chunk)
        finish(stud_moves)
        if number + 1 < bits:
            stud_moves = along_proto(1, stud_buf, number + 1)
    round_rows(stud_buf, stud)
    stud_t[...] = stud[...].T
    finish(weight_moves)
    weight = jnp.concatenate([weight_buf[i] for i in range(nb)], axis=1)

    def reduce(sweep, value, pbuf, qbuf, beside):
        pbuf[p] = value
        copies = []
        for d in range(1, np_):
            copies.append(pltpu.make_async_remote_copy(
                src_ref=pbuf.at[p], dst_ref=pbuf.at[p], send_sem=psend.at[sweep, d], recv_sem=precv.at[sweep, d],
                device_id=(b, lax.rem(p + d, np_)), device_id_type=MESH))
        for copy in copies:
            copy.start()
        beside(2 * sweep)
        finish(copies)
        total = pbuf[0]
        for d in range(1, np_):
            total = total + pbuf[d]
        qbuf[b] = total
        copies = []
        for d in range(1, nb):
            copies.append(pltpu.make_async_remote_copy(
                src_ref=qbuf.at[b], dst_ref=qbuf.at[b], send_sem=qsend.at[sweep, d], recv_sem=qrecv.at[sweep, d],
                device_id=(lax.rem(b + d, nb), p), device_id_type=MESH))
        for copy in copies:
            copy.start()
        beside(2 * sweep + 1)
        finish(copies)
        total = qbuf[0]
        for d in range(1, nb):
            total = total + qbuf[d]
        return total

    gaps = 2 * (SWEEPS - 1)

    def beside(gap):
        if gap < gaps:
            loop(chunks * gap // gaps, chunks * (gap + 1) // gaps, stud_chunk)

    scale = 1.0 / reduce(0, jnp.sum(acc[...], axis=0, keepdims=True), p0, q0, beside)
    for sweep in range(1, SWEEPS):
        last = scale
        wide = jnp.broadcast_to(scale, (8, rows))

        def body(i, row):
            for g in range(0, 128, 8):
                at = pl.ds(pl.multiple_of(i * 128 + g, 8), 8)
                e = energy[at, :]
                scaled = e * (1.0 / jnp.sum(e * wide, axis=1, keepdims=True))
                if sweep == SWEEPS - 1:
                    energy[at, :] = scaled
                row = row + scaled
            return row

        row = jnp.sum(lax.fori_loop(0, cols // 128, body, jnp.zeros((8, rows), jnp.float32)), axis=0, keepdims=True)
        if sweep == SWEEPS - 1:
            row = jnp.concatenate([row, jnp.sum(acc2[...], axis=0, keepdims=True)], axis=1)
        total = reduce(sweep, row, (p0, p1, p2)[sweep], (q0, q1, q2)[sweep], beside)
        scale = 1.0 / total[:, :rows]
    acc[0:1, :] = last
    acc[1:2, :] = scale * weight
    acc[2:3, :] = weight / total[:, rows:]
    scale_prev, target_scale, soft_scale = acc[0:1, :], acc[1:2, :], acc[2:3, :]
    keep = stud_t[pl.ds(pl.multiple_of(mine * 2 * block, 2 * block), 2 * block), :]
    keep_own = stud_t[pl.ds(pl.multiple_of(b * block, block), block), :]

    def to_other(turn, at):
        return pltpu.make_async_remote_copy(
            src_ref=away.at[:, at], dst_ref=out.at[:, at], send_sem=asend.at[turn], recv_sem=arecv.at[turn],
            device_id=(other, p), device_id_type=MESH)

    def to_result(turn, at):
        return pltpu.make_async_copy(own.at[:, at], out.at[:, at], osem.at[turn])

    def gradient(i, which, known):
        s, t, grad = sbufs[which], tbufs[which], gbufs[which]
        for g in range(0, step, 16):
            if known:
                scaled = energy[pl.ds(pl.multiple_of(i * step + g, 16), 16), :]
            else:
                e = jnp.exp2(t[g:g + 16, :] * (25.0 * LOG2E))
                scaled = e * (1.0 / jnp.sum(e * scale_prev, axis=1, keepdims=True))
            soft = jnp.exp2(s[g:g + 16, :] * (10.0 * LOG2E)) * soft_scale
            grad[g:g + 16, :] = (soft - scaled * target_scale).astype(jnp.bfloat16)

    def products(start, i, which, paired, alone):
        at = columns(start, i)
        grad = gbufs[which]
        if paired:
            res = dot_nt(keep, grad[...])
            low, high = res[:block], res[block:]
            own[:, at] = jnp.where(h == 0, low, high)
            away[:, at] = jnp.where(h == 0, high, low)
        else:
            own[:, at] = dot_nt(keep_own, grad[...])
        if not alone:
            part = grad[:, pl.ds(pl.multiple_of(mine * pair_rows, pair_rows), pair_rows)]
            back[...] += jnp.dot(wbuf[:, at], part, preferred_element_type=jnp.float32)

    def prepare(start, i, which, known):
        wt = pick(start, i)
        sbufs[which][...] = dot_nt(wt, stud[...])
        if not known:
            tbufs[which][...] = dot_nt(wt, teach[...])

    def run(turn, start, low, high, known, paired, alone=False):
        def send(i):
            at = columns(start, i)
            if paired:
                to_other(turn, at).start()
            to_result(turn, at).start()

        if high == low:
            return
        if (high - low) % 2 == 0:
            prepare(start, low, 0, known)

            def body(j, carry):
                i = low + 2 * j
                prepare(start, i + 1, 1, known)
                gradient(i, 0, known)
                products(start, i, 0, paired, alone)
                prepare(start, low + lax.rem(2 * j + 2, high - low), 0, known)
                gradient(i + 1, 1, known)
                products(start, i + 1, 1, paired, alone)
                send(i)
                send(i + 1)
                return carry

            lax.fori_loop(0, (high - low) // 2, body, 0)
        else:
            def body(j, carry):
                prepare(start, low + j, 0, known)
                gradient(low + j, 0, known)
                products(start, low + j, 0, paired, alone)
                send(low + j)
                return carry

            lax.fori_loop(0, high - low, body, 0)

    sent = chunks - twice
    starts = [lax.rem(mine + turn, quarters) * cols for turn in range(quarters)]
    run(0, base + starts[0], 0, chunks, True, True)
    for turn in range(1, quarters):
        run(turn, base + starts[turn], 0, sent, False, True)
    for turn in range(1, quarters):
        run(turn, base + starts[turn], sent, chunks, False, False)

    full = back[...].T
    for s in range(2 * np_):
        parts[s, 0:share, :] = full[s * share:(s + 1) * share, :]
    copies = []
    slot = h * np_ + p
    for d in range(1, 2 * np_):
        to = lax.rem(slot + d, 2 * np_)
        copies.append(pltpu.make_async_remote_copy(
            src_ref=parts.at[to], dst_ref=mine_buf.at[d], send_sem=bsend.at[d], recv_sem=brecv.at[d],
            device_id=(pair + to // np_, lax.rem(to, np_)), device_id_type=MESH))
    for copy in copies:
        copy.start()
    there = half - base
    for turn in range(1, quarters):
        run(quarters + turn, there + starts[turn], sent, chunks, False, False, True)
    total = parts[slot]
    finish(copies)
    for d in range(1, 2 * np_):
        total = total + mine_buf[d]
    unit = stud_own[...]
    full_back = inverse[...] * (total - unit * jnp.sum(unit * total, axis=1, keepdims=True))
    feature[...] = full_back[:share]
    for turn in range(quarters):
        span = cols if turn == 0 else sent * step
        to_result(turn, pl.ds(pl.multiple_of(base + starts[turn], cols), cols)).wait()
        if span > 0:
            to_other(turn, pl.ds(pl.multiple_of(base + starts[turn], cols), span)).wait_send()
            to_other(turn, pl.ds(pl.multiple_of(there + starts[turn], cols), span)).wait_recv()
        if turn > 0 and twice > 0:
            to_result(quarters + turn, pl.ds(pl.multiple_of(there + starts[turn] + sent * step, step), twice * step)).wait()


def on_device(nb, np_, teacher, student, perm, counts, prototypes):
    img_count = teacher.shape[0]
    patches = teacher.shape[1]
    width = teacher.shape[2]
    group_rows = GROUP_ROWS
    rows = nb * group_rows
    share = group_rows // np_
    pad = -(-share // 8) * 8
    local = prototypes.shape[1]
    p = lax.axis_index("proto")
    tally = counts.reshape(-1)
    order = jnp.arange(img_count, dtype=jnp.int32)
    ends = jnp.sum(jnp.where(order[None, :] <= order[:, None], tally[None, :], 0), axis=1)
    starts = ends - tally
    line = jnp.arange(group_rows, dtype=jnp.int32)
    owner = jnp.sum((ends[None, :] <= line[:, None]).astype(jnp.int32), axis=1)
    picked = owner[:, None] == jnp.arange(img_count, dtype=jnp.int32)[None, :]
    first = jnp.sum(jnp.where(picked, starts[None, :], 0), axis=1)
    owned = jnp.sum(jnp.where(picked, tally[None, :], 0), axis=1)
    weight = ((K * 10.0) * (1.0 / owned.astype(jnp.float32))).reshape(1, group_rows)
    place = lax.dynamic_slice_in_dim(owner * patches + line - first, p * share, share, 0)
    image = lax.dynamic_slice_in_dim(owner * patches, p * share, share, 0)
    flat = image + jnp.take(perm.reshape(-1), place)
    teach_unit, unused = unit_rows(jnp.take(teacher.reshape(-1, width), flat, axis=0))
    own_unit, own_inverse = unit_rows(jnp.take(student.reshape(-1, width), flat, axis=0))
    fill = lambda x: jnp.pad(x, ((0, pad - share), (0, 0))) if pad > share else x

    cols = local // nb
    step = min(256, cols)
    quarters = nb // 2
    twice = cols // step // 2
    block = width // nb
    pair_rows = 2 * group_rows
    vmem = pltpu.VMEM
    f32, bf16 = jnp.float32, jnp.bfloat16
    dma = pltpu.SemaphoreType.DMA
    whole = pl.BlockSpec(memory_space=vmem)
    proto_grad, feature_grad = pl.pallas_call(
        functools.partial(head_kernel, nb, np_, share, cols, step, twice),
        out_shape=[jax.ShapeDtypeStruct((block, local), f32), jax.ShapeDtypeStruct((share, width), f32)],
        in_specs=[whole, whole, whole, whole, pl.BlockSpec(memory_space=pl.ANY)],
        out_specs=[pl.BlockSpec(memory_space=pl.ANY), whole],
        scratch_shapes=[
            vmem((np_, nb, pad, width), f32), vmem((np_, nb, pad, width), f32), vmem((nb, 1, group_rows), f32),
            vmem((rows, width), bf16), vmem((rows, width), bf16), vmem((width, rows), bf16),
            vmem((group_rows, width), f32), vmem((cols, rows), f32), vmem((width, local), bf16),
            vmem((step, rows), f32), vmem((step, rows), f32), vmem((step, rows), f32), vmem((step, rows), f32),
            vmem((step, rows), bf16), vmem((step, rows), bf16),
            vmem((8, rows), f32), vmem((8, rows), f32),
            vmem((block, local), f32), vmem((block, local), f32),
            vmem((width, pair_rows), f32), vmem((2 * np_, pad, width), f32), vmem((2 * np_, pad, width), f32),
            vmem((np_, 1, rows), f32), vmem((np_, 1, rows), f32), vmem((np_, 1, 2 * rows), f32),
            vmem((nb, 1, rows), f32), vmem((nb, 1, rows), f32), vmem((nb, 1, 2 * rows), f32),
            dma, dma((2 * quarters,)), dma((quarters,)), dma((quarters,)), dma((2 * np_,)), dma((2 * np_,)),
            dma((SWEEPS, np_)), dma((SWEEPS, np_)), dma((SWEEPS, nb)), dma((SWEEPS, nb)),
            dma((3, nb)), dma((3, nb)), dma((2, 2, np_)), dma((2, 2, np_)),
        ],
        compiler_params=pltpu.CompilerParams(collective_id=0, has_side_effects=True, vmem_limit_bytes=60 * 2**20),
        name="head",
    )(fill(teach_unit), fill(own_unit), fill(own_inverse), weight, prototypes)
    return (feature_grad, proto_grad)


def solution(mesh):
    in_specs = (
        P("batch", None, None),
        P("batch", None, None),
        P("batch", None),
        P("batch", None),
        P(None, "proto"),
    )
    out_specs = (P(("batch", "proto"), None), P("batch", "proto"))
    run = functools.partial(on_device, mesh.shape["batch"], mesh.shape["proto"])
    return jax.shard_map(run, mesh=mesh, in_specs=in_specs, out_specs=out_specs, check_vma=False)
```

```python
import functools
import jax
import jax.numpy as jnp
from jax import lax
from jax.experimental import pallas as pl
from jax.experimental.pallas import tpu as pltpu
from jax.sharding import PartitionSpec as P

K = 131072
SWEEPS = 3
GROUP_ROWS = 384
LOG2E = 1.4426950408889634
MESH = pl.DeviceIdType.MESH
NT = (((1,), (1,)), ((), ()))


def unit_rows(rows):
    values = rows.astype(jnp.float32)
    inverse = lax.rsqrt(jnp.sum(values * values, axis=1, keepdims=True) + 1e-06)
    return (values * inverse, inverse)


def flip(index, bit):
    size = 2 ** bit
    return index + size - 2 * size * lax.rem(index // size, 2)


def dot_nt(left, right):
    return lax.dot_general(left, right, NT, preferred_element_type=jnp.float32)


def head_kernel(nb, np_, share, cols, step, twice, teach_own, stud_own, inverse, weight_own, proto, out, feature,
                teach_buf, stud_buf, weight_buf, teach, stud, stud_t, stage, energy, wbuf, ta, tb, sa, sb, ga, gb,
                acc, acc2, own, away, back, parts, mine_buf, p0, p1, p2, q0, q1, q2,
                wsem, osem, asend, arecv, bsend, brecv, psend, precv, qsend, qrecv,
                zsend, zrecv, gsend, grecv):
    b, p = lax.axis_index("batch"), lax.axis_index("proto")
    rows = teach.shape[0]
    group_rows = rows // nb
    bits = np_.bit_length() - 1
    h = lax.rem(b, 2)
    pair = b - h
    other = pair + 1 - h
    quarters = nb // 2
    mine = b // 2
    half = cols * quarters
    base = h * half
    block = out.shape[0]
    pair_rows = 2 * group_rows
    chunks = cols // step
    load = pltpu.make_async_copy(proto, wbuf, wsem)
    load.start()
    barrier = pltpu.get_barrier_semaphore()
    for d in range(1, np_):
        peer = lax.rem(p + d, np_)
        pl.semaphore_signal(barrier, inc=1, device_id=(b, peer), device_id_type=MESH)
        pl.semaphore_signal(barrier, inc=1, device_id=(other, peer), device_id_type=MESH)
    for d in range(1, nb):
        pl.semaphore_signal(barrier, inc=1, device_id=(lax.rem(b + d, nb), p), device_id_type=MESH)
    teach_buf[p, b] = teach_own[...]
    stud_buf[p, b] = stud_own[...]
    weight_buf[b] = weight_own[...]
    pl.semaphore_wait(barrier, 2 * (np_ - 1) + nb - 1)

    def along_batch(which, ref):
        copies = []
        for d in range(1, nb):
            copies.append(pltpu.make_async_remote_copy(
                src_ref=ref, dst_ref=ref, send_sem=zsend.at[which, d], recv_sem=zrecv.at[which, d],
                device_id=(lax.rem(b + d, nb), p), device_id_type=MESH))
        for copy in copies:
            copy.start()
        return copies

    def along_proto(which, buf, number):
        copies = []
        for part in range(2):
            outer = list(range(1, bits))
            order = (outer if part == 0 else outer[::-1]) + [0]
            held = [p]
            for bit in order[:number]:
                held = held + [flip(q, bit) for q in held]
            for k, slot in enumerate(held):
                ref = buf.at[slot, pl.ds(part * (nb // 2), nb // 2)]
                at = 2 ** number - 1 + k
                copies.append(pltpu.make_async_remote_copy(
                    src_ref=ref, dst_ref=ref, send_sem=gsend.at[which, part, at], recv_sem=grecv.at[which, part, at],
                    device_id=(b, flip(p, order[number])), device_id_type=MESH))
        for copy in copies:
            copy.start()
        return copies

    def finish(copies):
        for copy in copies:
            copy.wait()

    def round_rows(buf, target):
        for i in range(nb):
            for q in range(np_):
                stage[q * share:(q + 1) * share, :] = buf[q, i, 0:share, :]
            target[i * group_rows:(i + 1) * group_rows, :] = stage[...].astype(jnp.bfloat16)

    teach_moves = along_batch(0, teach_buf.at[p, b])
    for number in range(bits):
        finish(teach_moves)
        teach_moves = along_proto(0, teach_buf, number)
        if number == 0:
            stud_moves = along_batch(1, stud_buf.at[p, b])
            weight_moves = along_batch(2, weight_buf.at[b])
    load.wait()
    finish(stud_moves)
    finish(teach_moves)
    stud_moves = along_proto(1, stud_buf, 0)
    round_rows(teach_buf, teach)
    acc[...] = jnp.zeros_like(acc)
    acc2[...] = jnp.zeros_like(acc2)
    back[...] = jnp.zeros_like(back)

    def columns(start, i):
        return pl.ds(pl.multiple_of(start + i * step, step), step)

    def pick(start, i):
        return wbuf[:, columns(start, i)].T

    first = base + mine * cols

    def loop(low, high, one):
        if (high - low) % 2 == 0:
            def body(j, carry):
                one(low + 2 * j, 0)
                one(low + 2 * j + 1, 1)
                return carry
            lax.fori_loop(0, (high - low) // 2, body, 0)
        else:
            def body(j, carry):
                one(low + j, 0)
                return carry
            lax.fori_loop(0, high - low, body, 0)

    tbufs, sbufs, gbufs = (ta, tb), (sa, sb), (ga, gb)

    def teach_chunk(i, which):
        buf = tbufs[which]
        buf[...] = dot_nt(pick(first, i), teach[...])
        row = acc[...]
        for g in range(0, step, 8):
            e = jnp.exp2(buf[g:g + 8, :] * (25.0 * LOG2E))
            energy[pl.ds(pl.multiple_of(i * step + g, 8), 8), :] = e
            row = row + e * (1.0 / jnp.sum(e, axis=1, keepdims=True))
        acc[...] = row

    def stud_chunk(i, which):
        buf = sbufs[which]
        buf[...] = dot_nt(pick(first, i), stud[...])
        row = acc2[...]
        for g in range(0, step, 8):
            row = row + jnp.exp2(buf[g:g + 8, :] * (10.0 * LOG2E))
        acc2[...] = row

    for number in range(bits):
        loop(chunks * number // bits, chunks * (number + 1) // bits, teach_chunk)
        finish(stud_moves)
        if number + 1 < bits:
            stud_moves = along_proto(1, stud_buf, number + 1)
    round_rows(stud_buf, stud)
    stud_t[...] = stud[...].T
    finish(weight_moves)
    weight = jnp.concatenate([weight_buf[i] for i in range(nb)], axis=1)

    def reduce(sweep, value, pbuf, qbuf, beside):
        pbuf[p] = value
        copies = []
        for d in range(1, np_):
            copies.append(pltpu.make_async_remote_copy(
                src_ref=pbuf.at[p], dst_ref=pbuf.at[p], send_sem=psend.at[sweep, d], recv_sem=precv.at[sweep, d],
                device_id=(b, lax.rem(p + d, np_)), device_id_type=MESH))
        for copy in copies:
            copy.start()
        beside(2 * sweep)
        finish(copies)
        total = pbuf[0]
        for d in range(1, np_):
            total = total + pbuf[d]
        qbuf[b] = total
        copies = []
        for d in range(1, nb):
            copies.append(pltpu.make_async_remote_copy(
                src_ref=qbuf.at[b], dst_ref=qbuf.at[b], send_sem=qsend.at[sweep, d], recv_sem=qrecv.at[sweep, d],
                device_id=(lax.rem(b + d, nb), p), device_id_type=MESH))
        for copy in copies:
            copy.start()
        beside(2 * sweep + 1)
        finish(copies)
        total = qbuf[0]
        for d in range(1, nb):
            total = total + qbuf[d]
        return total

    gaps = 2 * (SWEEPS - 1)

    def beside(gap):
        if gap < gaps:
            loop(chunks * gap // gaps, chunks * (gap + 1) // gaps, stud_chunk)

    scale = 1.0 / reduce(0, jnp.sum(acc[...], axis=0, keepdims=True), p0, q0, beside)
    for sweep in range(1, SWEEPS):
        last = scale
        wide = jnp.broadcast_to(scale, (8, rows))

        def body(i, row):
            for g in range(0, 128, 8):
                at = pl.ds(pl.multiple_of(i * 128 + g, 8), 8)
                e = energy[at, :]
                scaled = e * (1.0 / jnp.sum(e * wide, axis=1, keepdims=True))
                row = row + scaled
            return row

        row = jnp.sum(lax.fori_loop(0, cols // 128, body, jnp.zeros((8, rows), jnp.float32)), axis=0, keepdims=True)
        if sweep == SWEEPS - 1:
            row = jnp.concatenate([row, jnp.sum(acc2[...], axis=0, keepdims=True)], axis=1)
        total = reduce(sweep, row, (p0, p1, p2)[sweep], (q0, q1, q2)[sweep], beside)
        scale = 1.0 / total[:, :rows]
    acc[0:1, :] = last
    acc[1:2, :] = scale * weight
    acc[2:3, :] = weight / total[:, rows:]
    scale_prev, target_scale, soft_scale = acc[0:1, :], acc[1:2, :], acc[2:3, :]
    keep = stud_t[pl.ds(pl.multiple_of(mine * 2 * block, 2 * block), 2 * block), :]
    keep_own = stud_t[pl.ds(pl.multiple_of(b * block, block), block), :]

    def to_other(turn, at):
        return pltpu.make_async_remote_copy(
            src_ref=away.at[:, at], dst_ref=out.at[:, at], send_sem=asend.at[turn], recv_sem=arecv.at[turn],
            device_id=(other, p), device_id_type=MESH)

    def to_result(turn, at):
        return pltpu.make_async_copy(own.at[:, at], out.at[:, at], osem.at[turn])

    def gradient(i, which, known):
        s, t, grad = sbufs[which], tbufs[which], gbufs[which]

        def held(g):
            return energy[pl.ds(pl.multiple_of(i * step + g, 16), 16), :] if known else t[g:g + 16, :]

        col_scale = []
        for g in range(0, step, 16):
            if known:
                e = held(g)
            else:
                e = jnp.exp2(t[g:g + 16, :] * (25.0 * LOG2E))
                t[g:g + 16, :] = e
            col_scale.append(1.0 / jnp.sum(e * scale_prev, axis=1, keepdims=True))
        for g in range(0, step, 16):
            soft = jnp.exp2(s[g:g + 16, :] * (10.0 * LOG2E)) * soft_scale
            grad[g:g + 16, :] = (soft - held(g) * target_scale * col_scale[g // 16]).astype(jnp.bfloat16)

    def products(start, i, which, paired, alone):
        at = columns(start, i)
        grad = gbufs[which]
        if paired:
            res = dot_nt(keep, grad[...])
            low, high = res[:block], res[block:]
            own[:, at] = jnp.where(h == 0, low, high)
            away[:, at] = jnp.where(h == 0, high, low)
        else:
            own[:, at] = dot_nt(keep_own, grad[...])
        if not alone:
            part = grad[:, pl.ds(pl.multiple_of(mine * pair_rows, pair_rows), pair_rows)]
            back[...] += jnp.dot(wbuf[:, at], part, preferred_element_type=jnp.float32)

    def prepare(start, i, which, known):
        wt = pick(start, i)
        sbufs[which][...] = dot_nt(wt, stud[...])
        if not known:
            tbufs[which][...] = dot_nt(wt, teach[...])

    def run(turn, start, low, high, known, paired, alone=False):
        def send(i):
            at = columns(start, i)
            if paired:
                to_other(turn, at).start()
            to_result(turn, at).start()

        if high == low:
            return
        if (high - low) % 2 == 0:
            prepare(start, low, 0, known)

            def body(j, carry):
                i = low + 2 * j
                prepare(start, i + 1, 1, known)
                gradient(i, 0, known)
                products(start, i, 0, paired, alone)
                prepare(start, low + lax.rem(2 * j + 2, high - low), 0, known)
                gradient(i + 1, 1, known)
                products(start, i + 1, 1, paired, alone)
                send(i)
                send(i + 1)
                return carry

            lax.fori_loop(0, (high - low) // 2, body, 0)
        else:
            def body(j, carry):
                prepare(start, low + j, 0, known)
                gradient(low + j, 0, known)
                products(start, low + j, 0, paired, alone)
                send(low + j)
                return carry

            lax.fori_loop(0, high - low, body, 0)

    sent = chunks - twice
    starts = [lax.rem(mine + turn, quarters) * cols for turn in range(quarters)]
    run(0, base + starts[0], 0, chunks, True, True)
    for turn in range(1, quarters):
        run(turn, base + starts[turn], 0, sent, False, True)
    for turn in range(1, quarters):
        run(turn, base + starts[turn], sent, chunks, False, False)

    full = back[...].T
    for s in range(2 * np_):
        parts[s, 0:share, :] = full[s * share:(s + 1) * share, :]
    copies = []
    slot = h * np_ + p
    for d in range(1, 2 * np_):
        to = lax.rem(slot + d, 2 * np_)
        copies.append(pltpu.make_async_remote_copy(
            src_ref=parts.at[to], dst_ref=mine_buf.at[d], send_sem=bsend.at[d], recv_sem=brecv.at[d],
            device_id=(pair + to // np_, lax.rem(to, np_)), device_id_type=MESH))
    for copy in copies:
        copy.start()
    there = half - base
    for turn in range(1, quarters):
        run(quarters + turn, there + starts[turn], sent, chunks, False, False, True)
    total = parts[slot]
    finish(copies)
    for d in range(1, 2 * np_):
        total = total + mine_buf[d]
    unit = stud_own[...]
    full_back = inverse[...] * (total - unit * jnp.sum(unit * total, axis=1, keepdims=True))
    feature[...] = full_back[:share]
    for turn in range(quarters):
        span = cols if turn == 0 else sent * step
        to_result(turn, pl.ds(pl.multiple_of(base + starts[turn], cols), cols)).wait()
        if span > 0:
            to_other(turn, pl.ds(pl.multiple_of(base + starts[turn], cols), span)).wait_send()
            to_other(turn, pl.ds(pl.multiple_of(there + starts[turn], cols), span)).wait_recv()
        if turn > 0 and twice > 0:
            to_result(quarters + turn, pl.ds(pl.multiple_of(there + starts[turn] + sent * step, step), twice * step)).wait()


def on_device(nb, np_, teacher, student, perm, counts, prototypes):
    img_count = teacher.shape[0]
    patches = teacher.shape[1]
    width = teacher.shape[2]
    group_rows = GROUP_ROWS
    rows = nb * group_rows
    share = group_rows // np_
    pad = -(-share // 8) * 8
    local = prototypes.shape[1]
    p = lax.axis_index("proto")
    tally = counts.reshape(-1)
    order = jnp.arange(img_count, dtype=jnp.int32)
    ends = jnp.sum(jnp.where(order[None, :] <= order[:, None], tally[None, :], 0), axis=1)
    starts = ends - tally
    line = jnp.arange(group_rows, dtype=jnp.int32)
    owner = jnp.sum((ends[None, :] <= line[:, None]).astype(jnp.int32), axis=1)
    picked = owner[:, None] == jnp.arange(img_count, dtype=jnp.int32)[None, :]
    first = jnp.sum(jnp.where(picked, starts[None, :], 0), axis=1)
    owned = jnp.sum(jnp.where(picked, tally[None, :], 0), axis=1)
    weight = ((K * 10.0) * (1.0 / owned.astype(jnp.float32))).reshape(1, group_rows)
    place = lax.dynamic_slice_in_dim(owner * patches + line - first, p * share, share, 0)
    image = lax.dynamic_slice_in_dim(owner * patches, p * share, share, 0)
    flat = image + jnp.take(perm.reshape(-1), place)
    teach_unit, unused = unit_rows(jnp.take(teacher.reshape(-1, width), flat, axis=0))
    own_unit, own_inverse = unit_rows(jnp.take(student.reshape(-1, width), flat, axis=0))
    fill = lambda x: jnp.pad(x, ((0, pad - share), (0, 0))) if pad > share else x

    cols = local // nb
    step = min(256, cols)
    quarters = nb // 2
    twice = cols // step // 4
    block = width // nb
    pair_rows = 2 * group_rows
    vmem = pltpu.VMEM
    f32, bf16 = jnp.float32, jnp.bfloat16
    dma = pltpu.SemaphoreType.DMA
    whole = pl.BlockSpec(memory_space=vmem)
    proto_grad, feature_grad = pl.pallas_call(
        functools.partial(head_kernel, nb, np_, share, cols, step, twice),
        out_shape=[jax.ShapeDtypeStruct((block, local), f32), jax.ShapeDtypeStruct((share, width), f32)],
        in_specs=[whole, whole, whole, whole, pl.BlockSpec(memory_space=pl.ANY)],
        out_specs=[pl.BlockSpec(memory_space=pl.ANY), whole],
        scratch_shapes=[
            vmem((np_, nb, pad, width), f32), vmem((np_, nb, pad, width), f32), vmem((nb, 1, group_rows), f32),
            vmem((rows, width), bf16), vmem((rows, width), bf16), vmem((width, rows), bf16),
            vmem((group_rows, width), f32), vmem((cols, rows), f32), vmem((width, local), bf16),
            vmem((step, rows), f32), vmem((step, rows), f32), vmem((step, rows), f32), vmem((step, rows), f32),
            vmem((step, rows), bf16), vmem((step, rows), bf16),
            vmem((8, rows), f32), vmem((8, rows), f32),
            vmem((block, local), f32), vmem((block, local), f32),
            vmem((width, pair_rows), f32), vmem((2 * np_, pad, width), f32), vmem((2 * np_, pad, width), f32),
            vmem((np_, 1, rows), f32), vmem((np_, 1, rows), f32), vmem((np_, 1, 2 * rows), f32),
            vmem((nb, 1, rows), f32), vmem((nb, 1, rows), f32), vmem((nb, 1, 2 * rows), f32),
            dma, dma((2 * quarters,)), dma((quarters,)), dma((quarters,)), dma((2 * np_,)), dma((2 * np_,)),
            dma((SWEEPS, np_)), dma((SWEEPS, np_)), dma((SWEEPS, nb)), dma((SWEEPS, nb)),
            dma((3, nb)), dma((3, nb)), dma((2, 2, np_)), dma((2, 2, np_)),
        ],
        compiler_params=pltpu.CompilerParams(collective_id=0, has_side_effects=True, vmem_limit_bytes=60 * 2**20),
        name="head",
    )(fill(teach_unit), fill(own_unit), fill(own_inverse), weight, prototypes)
    return (feature_grad, proto_grad)


def solution(mesh):
    in_specs = (
        P("batch", None, None),
        P("batch", None, None),
        P("batch", None),
        P("batch", None),
        P(None, "proto"),
    )
    out_specs = (P(("batch", "proto"), None), P("batch", "proto"))
    run = functools.partial(on_device, mesh.shape["batch"], mesh.shape["proto"])
    return jax.shard_map(run, mesh=mesh, in_specs=in_specs, out_specs=out_specs, check_vma=False)
```
